32 devices in a mesh: pw: 2 (over y), row: 4 (over z), col: 4 (over x, core).
Axes of the slice: x: 2, y: 2, z: 4, core: 2. Of those that a mesh axis runs over, the one named last changes fastest.
Arguments:
- pair_density: bfloat16 [2048, 2, 12288], P(('row', 'col'), None, 'pw'), may hold values from -0.25 to 0.25
- coulomb: float32 [12288], P('pw'), may hold values from 0.05 to 5
- valence_band: int32 [2048], P(('row', 'col')), may hold values from 0 to 511
- conduction_band: int32 [2048], P(('row', 'col')), may hold values from 0 to 31
- valence_energy: float32 [512], replicated, may hold values from -9 to -1
- conduction_energy: float32 [32], replicated, may hold values from 1 to 6
Outputs:
- hamiltonian: float32 [4, 4, 128, 2, 4, 4, 128], P('row', None, 'pw', None, None, 'col')
The draws below stay inside these ranges and needn't reach their ends.
All inputs are finite; a program needn't handle non-finite values.
Results may differ from the reference program's by a relative error of at most 0.0003.
Values sent between devices are 32-bit elements; how exact they have to be, the bound alone decides.
A program may use at most 128 MiB of HBM per device.

```python
import math
import jax
import jax.numpy as jnp
from jax import lax

NG = 12288
TDEV = 128
NV = 512
NC = 32
NT = 2048
N_ROW = 4
N_COL = 4


def set_ends(values, rng, least, high):
    spot = [jax.random.randint(jax.random.fold_in(rng, axis), (), 0, length) for axis, length in enumerate(values.shape)]
    main_axis = values.shape.index(max(values.shape))
    beside = spot[:main_axis] + [(spot[main_axis] + 1) % values.shape[main_axis]] + spot[main_axis + 1:]
    return values.at[tuple(spot)].set(least).at[tuple(beside)].set(high)


def block_levels(own_key, dims, split, low, largest):
    gain, own = 1.0, jax.random.fold_in(own_key, 6)
    for position, blocks in split:
        draws = jnp.exp(jax.random.uniform(jax.random.fold_in(own, position), (blocks,), jnp.float32, low / len(split), largest / len(split)))
        gain = gain * jnp.repeat(draws, dims[position] // blocks).reshape([-1 if axis == position else 1 for axis in range(len(dims))])
    return gain


def gaussian(stream_key, shape, width, bound, shards=(), kind=jnp.bfloat16):
    values = jax.random.normal(stream_key, shape, jnp.float32) * width
    if len(shards) > 0:
        values = block_levels(stream_key, shape, shards, -0.22, 0.18) * values
    return jnp.clip(values, min=-bound, max=bound).astype(kind)


def setup_inputs(seed: int = 0) -> dict:
    streams_of = jax.random.split(jax.random.key(seed), 7)
    pair_density = gaussian(streams_of[0], (NT, 2, NG), 0.045, 0.25, ((0, 16), (2, 2)))
    coulomb = jnp.clip(jnp.exp(math.log(5.0) - 4.6051702 * jax.random.uniform(streams_of[1], (NG,), jnp.float32) ** block_levels(streams_of[1], (NG,), ((0, 2),), -0.2, 0.2)), 0.05, 5.0)
    valence_band = set_ends(jax.random.randint(streams_of[2], (NT,), 0, NV), jax.random.fold_in(streams_of[2], 1), 0, NV - 1).astype(jnp.int32)
    conduction_band = set_ends(jax.random.randint(streams_of[3], (NT,), 0, NC), jax.random.fold_in(streams_of[3], 1), 0, NC - 1).astype(jnp.int32)
    valence_energy = jnp.clip(jax.random.uniform(streams_of[4], (NV,), jnp.float32, -9.0, -1.0), -9.0, -1.0)
    conduction_energy = jnp.clip(jax.random.uniform(streams_of[5], (NC,), jnp.float32, 1.0, 6.0), 1.0, 6.0)
    return dict(pair_density=pair_density, coulomb=coulomb, valence_band=valence_band, conduction_band=conduction_band, valence_energy=valence_energy, conduction_energy=conduction_energy)


def reference(pair_density, coulomb, valence_band, conduction_band, valence_energy, conduction_energy):
    scaled = jnp.sqrt(coulomb)[None, None, :] * pair_density.astype(jnp.float32)
    trans_count = scaled.shape[0]
    flat_rows = scaled.reshape(trans_count, -1)
    swapped = jnp.stack([scaled[:, 1, :], -scaled[:, 0, :]], axis=1).reshape(trans_count, -1)
    real_part = jnp.dot(flat_rows, flat_rows.T, precision=lax.Precision.HIGHEST, preferred_element_type=jnp.float32)
    imag_part = jnp.dot(flat_rows, swapped.T, precision=lax.Precision.HIGHEST, preferred_element_type=jnp.float32)
    gap = conduction_energy[conduction_band] - valence_energy[valence_band]
    real_part = 2.0 * real_part + jnp.diag(gap)
    imag_part = 2.0 * imag_part
    stacked = jnp.stack([real_part, imag_part], axis=0)
    shaped = stacked.reshape(2, N_ROW, N_COL, TDEV, N_ROW, N_COL, TDEV)
    return jnp.transpose(shaped, (1, 2, 3, 0, 4, 5, 6))
```

```python
import functools
import jax
import jax.numpy as jnp
from jax import lax
from jax.experimental import pallas as pl
from jax.experimental.pallas import tpu as pltpu
from jax.sharding import PartitionSpec as P

MESH = pl.DeviceIdType.MESH


def piece_width(depth):
    for width in (768, 512, 256):
        if depth % (2 * width) == 0:
            return width
    return 128


def kernel(
    rows, pieces, x_ref, c_ref, o_ref, panel, same, other, acc,
    p_recv, same_recv, other_recv, own_send, in_send, out_send,
):
    half = pieces // 2
    mid = rows // 2
    ahead = min(2, half)
    z = lax.axis_index("row")
    b = lax.axis_index("col")
    core = b + 1 - 2 * (b % 2)
    beside = (b + 2) % 4
    opposite = 3 - b
    side = z // mid
    m = z + side * (rows - 1 - 2 * z)
    step_in = 1 - 2 * side
    z_in = z + step_in
    z_out = z - step_in
    innermost = m == mid - 1
    cross_count = half * mid
    outer_count = 2 * half * m
    inner_sends = jnp.where(innermost, half * (m + 1), 2 * half * (m + 1))

    barrier = pltpu.get_barrier_semaphore()
    pl.semaphore_signal(barrier, inc=1, device_id={"col": core}, device_id_type=MESH)
    pl.semaphore_signal(barrier, inc=1, device_id={"col": beside}, device_id_type=MESH)
    pl.semaphore_signal(barrier, inc=1, device_id={"row": z_in}, device_id_type=MESH)

    @pl.when(m > 0)
    def _():
        pl.semaphore_signal(barrier, inc=1, device_id={"row": z_out}, device_id_type=MESH)
        pl.semaphore_wait(barrier, 4)

    @pl.when(m == 0)
    def _():
        pl.semaphore_wait(barrier, 3)

    def copy(src, dst, send, recv, where):
        return pltpu.make_async_remote_copy(
            src_ref=src, dst_ref=dst, send_sem=send, recv_sem=recv,
            device_id=where, device_id_type=MESH,
        )

    def arrived(slot, recv):
        copy(slot, slot, own_send.at[0, 0], recv, {"col": core}).wait_recv()

    def order(i):
        return (i + half) % pieces

    def send_own(i):
        q = order(i)
        copy(x_ref.at[q], panel.at[0, q], own_send.at[0, q], p_recv.at[0, q], {"col": core}).start()
        copy(x_ref.at[q], panel.at[1, q], own_send.at[1, q], p_recv.at[1, q], {"col": beside}).start()

    def send_inward(s):
        crossing = s < half * (m + 1)
        rest = jnp.where(crossing, s, s - half * (m + 1))
        back = rest // half
        chunk = m - back
        q = rest % half + jnp.where(crossing, 0, half)
        where = {"row": z_in}

        @pl.when(innermost & (back == 0))
        def _():
            copy(x_ref.at[q], other.at[chunk, q], in_send.at[s], other_recv.at[chunk, q], where).start()

        @pl.when(innermost & (back > 0))
        def _():
            copy(same.at[chunk, q], other.at[chunk, q], in_send.at[s], other_recv.at[chunk, q], where).start()

        @pl.when(jnp.logical_not(innermost) & (back == 0))
        def _():
            copy(x_ref.at[q], same.at[chunk, q], in_send.at[s], same_recv.at[chunk, q], where).start()

        if mid > 2:
            @pl.when(jnp.logical_not(innermost) & (back > 0))
            def _():
                copy(same.at[chunk, q], same.at[chunk, q], in_send.at[s], same_recv.at[chunk, q], where).start()

    def outer_arrival(u):
        crossing = u < half * m
        rest = jnp.where(crossing, u, u - half * m)
        return m - 1 - rest // half, rest % half + jnp.where(crossing, 0, half)

    def multiply(chunk, q, target):
        weighted = chunk[...] * c_ref[q]
        high = weighted.astype(jnp.bfloat16)
        low = (weighted - high.astype(jnp.float32)).astype(jnp.bfloat16)
        blocks = (x_ref.at[q], panel.at[0, q], panel.at[1, q], panel.at[2, q])
        dims = (((1,), (1,)), ((), ()))
        for block, a in zip(blocks, (b, core, beside, opposite)):
            left = block[...].astype(jnp.bfloat16)
            acc[target, a] += lax.dot_general(
                left, high, dims, preferred_element_type=jnp.float32
            ) + lax.dot_general(left, low, dims, preferred_element_type=jnp.float32)

    for i in range(ahead):
        send_own(i)
        send_inward(i)

    def clear(i, carry):
        acc[i // 4, i % 4] = jnp.zeros(acc.shape[2:], jnp.float32)
        return carry

    lax.fori_loop(0, rows * 4, clear, 0)
    lag = mid - 1 - m

    def step(t, carry):
        v = t - lag
        inner_here = (v >= 0) & (v < cross_count)
        v = jnp.clip(v, 0, cross_count - 1)
        inner_chunk, inner_q = mid - 1 - v // half, v % half

        @pl.when(t < outer_count)
        def _():
            chunk, q = outer_arrival(t)
            arrived(same.at[chunk, q], same_recv.at[chunk, q])

        @pl.when(t + ahead < inner_sends)
        def _():
            send_inward(t + ahead)

        @pl.when(t + ahead < pieces)
        def _():
            send_own(t + ahead)

        @pl.when(inner_here)
        def _():
            arrived(other.at[inner_chunk, inner_q], other_recv.at[inner_chunk, inner_q])

        @pl.when(inner_here & (m > 0))
        def _():
            copy(
                other.at[inner_chunk, inner_q], other.at[inner_chunk, inner_q],
                out_send.at[v], other_recv.at[inner_chunk, inner_q], {"row": z_out},
            ).start()

        @pl.when(t < pieces)
        def _():
            q = order(t)
            arrived(panel.at[1, q], p_recv.at[1, q])
            copy(
                panel.at[1, q], panel.at[2, q], own_send.at[2, q], p_recv.at[2, q], {"col": core}
            ).start()
            arrived(panel.at[0, q], p_recv.at[0, q])

        @pl.when((t >= 1) & (t <= pieces))
        def _():
            q = order(t - 1)
            arrived(panel.at[2, q], p_recv.at[2, q])
            multiply(x_ref.at[q], q, z)

        @pl.when((t >= half + 1) & (t - half - 1 < half * m))
        def _():
            chunk, q = outer_arrival(t - half - 1)
            multiply(same.at[chunk, q], q, chunk + side * (rows - 1 - 2 * chunk))

        @pl.when((t >= half * m) & (t < outer_count))
        def _():
            chunk, q = outer_arrival(t)
            multiply(same.at[chunk, q], q, chunk + side * (rows - 1 - 2 * chunk))

        w = t - 1 - lag

        @pl.when((w >= 0) & (w < cross_count))
        def _():
            chunk, q = mid - 1 - w // half, w % half
            multiply(other.at[chunk, q], q + half, chunk + (1 - side) * (rows - 1 - 2 * chunk))

        return carry

    steps = max(pieces + 1, cross_count + mid, 2 * half * (mid - 1))
    lax.fori_loop(0, steps, step, 0)

    def finish(i, carry):
        s, a = i // 4, i % 4
        n = acc.shape[2] // 2
        o_ref[s, a, 0] = 2.0 * (acc[s, a, :n, :n] + acc[s, a, n:, n:])
        o_ref[s, a, 1] = 2.0 * (acc[s, a, :n, n:] - acc[s, a, n:, :n])
        return carry

    lax.fori_loop(0, rows * 4, finish, 0)

    def left(send):
        copy(x_ref.at[0], panel.at[0, 0], send, p_recv.at[0, 0], {"col": core}).wait_send()

    def drain_own(i, carry):
        left(own_send.at[0, i])
        left(own_send.at[1, i])
        left(own_send.at[2, i])
        return carry

    lax.fori_loop(0, pieces, drain_own, 0)

    def drain_in(i, carry):
        @pl.when(i < inner_sends)
        def _():
            left(in_send.at[i])

        return carry

    lax.fori_loop(0, 2 * cross_count, drain_in, 0)

    @pl.when(m > 0)
    def _():
        def drain_out(i, carry):
            left(out_send.at[i])
            return carry

        lax.fori_loop(0, cross_count, drain_out, 0)


def partial_tiles(x, c, row_count):
    pieces, height, width = x.shape
    half, mid = pieces // 2, row_count // 2
    return pl.pallas_call(
        functools.partial(kernel, row_count, pieces),
        out_shape=jax.ShapeDtypeStruct((row_count, 4, 2, height // 2, height // 2), jnp.float32),
        in_specs=[pl.BlockSpec(memory_space=pltpu.VMEM)] * 2,
        out_specs=pl.BlockSpec(memory_space=pltpu.VMEM),
        scratch_shapes=[
            pltpu.VMEM((3, pieces, height, width), jnp.float32),
            pltpu.VMEM((max(mid - 1, 1), pieces, height, width), jnp.float32),
            pltpu.VMEM((mid, half, height, width), jnp.float32),
            pltpu.VMEM((row_count, 4, height, height), jnp.float32),
            pltpu.SemaphoreType.DMA((3, pieces)),
            pltpu.SemaphoreType.DMA((max(mid - 1, 1), pieces)),
            pltpu.SemaphoreType.DMA((mid, half)),
            pltpu.SemaphoreType.DMA((3, pieces)),
            pltpu.SemaphoreType.DMA((2 * half * mid,)),
            pltpu.SemaphoreType.DMA((half * mid,)),
        ],
        compiler_params=pltpu.CompilerParams(
            collective_id=0, has_side_effects=True, vmem_limit_bytes=56 * 2**20
        ),
    )(x, c)


def per_device(
    pair_density, coulomb, valence_band, conduction_band, valence_energy, conduction_energy
):
    tile_len, _, depth = pair_density.shape
    row_count = lax.axis_size("row")
    col_count = lax.axis_size("col")
    plane_count = lax.axis_size("pw")
    share_len = tile_len // plane_count
    row_here = lax.axis_index("row")
    col_here = lax.axis_index("col")
    plane_here = lax.axis_index("pw")
    assert col_count == 4 and row_count % 2 == 0

    width = piece_width(depth)
    pieces = depth // width
    far_side = row_here >= row_count // 2

    def from_side(array):
        return jnp.where(far_side, jnp.roll(array, pieces // 2, axis=0), array)

    x = jnp.transpose(pair_density.reshape(tile_len, 2, pieces, width), (2, 1, 0, 3))
    x = from_side(x.reshape(pieces, 2 * tile_len, width)).astype(jnp.float32)
    c = from_side(coulomb.reshape(pieces, 1, width))
    blocks = partial_tiles(x, c, row_count)

    def shares(plane):
        rows = lax.dynamic_slice_in_dim(blocks, plane * share_len, share_len, 3)
        cols = lax.dynamic_slice_in_dim(blocks, plane * share_len, share_len, 4)
        rows = jnp.transpose(rows, (1, 3, 2, 0, 4))
        cols = jnp.transpose(cols, (0, 1, 2, 4, 3))
        return rows, cols

    direct, outgoing = shares(plane_here)
    for distance in range(1, plane_count):
        route = [(i, (i + distance) % plane_count) for i in range(plane_count)]
        rows, cols = shares(jnp.remainder(plane_here + distance, plane_count))
        outgoing = outgoing + lax.ppermute(cols, "pw", route)
        direct = direct + lax.ppermute(rows, "pw", route)
    outgoing = outgoing.reshape(row_count * col_count, 2, share_len, tile_len)
    incoming = lax.all_to_all(outgoing, ("row", "col"), split_axis=0, concat_axis=0, tiled=True)
    incoming = incoming.reshape(row_count, col_count, 2, share_len, tile_len)
    conjugate = jnp.array([1.0, -1.0], jnp.float32)
    mirrored = jnp.transpose(incoming, (1, 3, 2, 0, 4)) * conjugate[None, None, :, None, None]
    elsewhere = (jnp.arange(row_count, dtype=jnp.int32) != row_here)[None, None, None, :, None]
    reduced = direct + jnp.where(elsewhere, mirrored, 0.0)
    own_valence = lax.dynamic_slice_in_dim(valence_band, plane_here * share_len, share_len, 0)
    own_conduction = lax.dynamic_slice_in_dim(conduction_band, plane_here * share_len, share_len, 0)
    valence_ids = jnp.arange(valence_energy.shape[0], dtype=jnp.int32)
    conduction_ids = jnp.arange(conduction_energy.shape[0], dtype=jnp.int32)
    upper_level = jnp.sum(
        jnp.where(
            own_conduction[:, None] == conduction_ids[None, :], conduction_energy[None, :], 0.0
        ),
        axis=1,
    )
    lower_level = jnp.sum(
        jnp.where(own_valence[:, None] == valence_ids[None, :], valence_energy[None, :], 0.0),
        axis=1,
    )
    gap = upper_level - lower_level
    col_match = (jnp.arange(col_count, dtype=jnp.int32) == col_here)[:, None, None, None, None]
    row_match = (jnp.arange(row_count, dtype=jnp.int32) == row_here)[None, None, None, :, None]
    real_match = (jnp.arange(2, dtype=jnp.int32) == 0)[None, None, :, None, None]
    inner_match = (
        jnp.arange(tile_len, dtype=jnp.int32)[None, None, None, None, :]
        == plane_here * share_len
        + jnp.arange(share_len, dtype=jnp.int32)[None, :, None, None, None]
    )
    on_diagonal = col_match & row_match & real_match & inner_match
    result = reduced + jnp.where(on_diagonal, gap[None, :, None, None, None], 0.0)
    return result.reshape(1, col_count, share_len, 2, row_count, 1, tile_len)


def solution(mesh):
    placed = (
        P(("row", "col"), None, "pw"),
        P("pw"),
        P(("row", "col")),
        P(("row", "col")),
        P(),
        P(),
    )
    return jax.shard_map(
        per_device,
        mesh=mesh,
        in_specs=placed,
        out_specs=P("row", None, "pw", None, None, "col", None),
        check_vma=False,
    )
```

```python
import functools
import jax
import jax.numpy as jnp
from jax import lax
from jax.experimental import pallas as pl
from jax.experimental.pallas import tpu as pltpu
from jax.sharding import PartitionSpec as P

MESH = pl.DeviceIdType.MESH


def piece_width(depth):
    for width in (256,):
        if depth % (2 * width) == 0:
            return width
    return 128


def kernel(
    rows, planes, pieces, x_ref, c_ref, direct_ref, outgoing_ref, panel, same, other, acc,
    tile, flipped, tile_in, flipped_in,
    p_recv, same_recv, other_recv, own_send, in_send, out_send, plane_recv, plane_send,
):
    half = pieces // 2
    mid = rows // 2
    ahead = min(2, half)
    z = lax.axis_index("row")
    b = lax.axis_index("col")
    core = b + 1 - 2 * (b % 2)
    beside = (b + 2) % 4
    opposite = 3 - b
    plane = lax.axis_index("pw")
    share = tile_in.shape[-2]
    side = z // mid
    m = z + side * (rows - 1 - 2 * z)
    step_in = 1 - 2 * side
    z_in = z + step_in
    z_out = z - step_in
    innermost = m == mid - 1
    cross_count = half * mid
    outer_count = 2 * half * m
    inner_sends = jnp.where(innermost, half * (m + 1), 2 * half * (m + 1))

    barrier = pltpu.get_barrier_semaphore()
    pl.semaphore_signal(barrier, inc=1, device_id={"col": core}, device_id_type=MESH)
    pl.semaphore_signal(barrier, inc=1, device_id={"col": beside}, device_id_type=MESH)
    pl.semaphore_signal(barrier, inc=1, device_id={"row": z_in}, device_id_type=MESH)

    for distance in range(1, planes):
        pl.semaphore_signal(
            barrier, inc=1, device_id={"pw": (plane + distance) % planes}, device_id_type=MESH
        )

    @pl.when(m > 0)
    def _():
        pl.semaphore_signal(barrier, inc=1, device_id={"row": z_out}, device_id_type=MESH)
        pl.semaphore_wait(barrier, 3 + planes)

    @pl.when(m == 0)
    def _():
        pl.semaphore_wait(barrier, 2 + planes)

    def copy(src, dst, send, recv, where):
        return pltpu.make_async_remote_copy(
            src_ref=src, dst_ref=dst, send_sem=send, recv_sem=recv,
            device_id=where, device_id_type=MESH,
        )

    def arrived(slot, recv):
        copy(slot, slot, own_send.at[0, 0], recv, {"col": core}).wait_recv()

    def order(i):
        return (i + half) % pieces

    def span(q):
        width = panel.shape[-1]
        place = (q + side * half) % pieces
        return pl.ds(pl.multiple_of(place * width, 128), width)

    def own(q):
        return x_ref.at[:, :, span(q)]

    def send_own(i):
        q = order(i)
        copy(own(q), panel.at[0, q], own_send.at[0, q], p_recv.at[0, q], {"col": core}).start()
        copy(own(q), panel.at[1, q], own_send.at[1, q], p_recv.at[1, q], {"col": beside}).start()

    def send_inward(s):
        crossing = s < half * (m + 1)
        rest = jnp.where(crossing, s, s - half * (m + 1))
        back = rest // half
        chunk = m - back
        q = rest % half + jnp.where(crossing, 0, half)
        where = {"row": z_in}

        @pl.when(innermost & (back == 0))
        def _():
            copy(own(q), other.at[chunk, q], in_send.at[s], other_recv.at[chunk, q], where).start()

        @pl.when(innermost & (back > 0))
        def _():
            copy(same.at[chunk, q], other.at[chunk, q], in_send.at[s], other_recv.at[chunk, q], where).start()

        @pl.when(jnp.logical_not(innermost) & (back == 0))
        def _():
            copy(own(q), same.at[chunk, q], in_send.at[s], same_recv.at[chunk, q], where).start()

        if mid > 2:
            @pl.when(jnp.logical_not(innermost) & (back > 0))
            def _():
                copy(same.at[chunk, q], same.at[chunk, q], in_send.at[s], same_recv.at[chunk, q], where).start()

    def outer_arrival(u):
        crossing = u < half * m
        rest = jnp.where(crossing, u, u - half * m)
        return m - 1 - rest // half, rest % half + jnp.where(crossing, 0, half)

    def multiply(chunk, q, target):
        weighted = chunk[...].reshape(acc.shape[2], -1) * c_ref[:, span(q)]
        high = weighted.astype(jnp.bfloat16)
        low = (weighted - high.astype(jnp.float32)).astype(jnp.bfloat16)
        blocks = (own(q), panel.at[0, q], panel.at[1, q], panel.at[2, q])
        dims = (((1,), (1,)), ((), ()))
        for block, a in zip(blocks, (b, core, beside, opposite)):
            left = block[...].reshape(acc.shape[2], -1).astype(jnp.bfloat16)
            acc[target, a] += lax.dot_general(
                left, high, dims, preferred_element_type=jnp.float32
            ) + lax.dot_general(left, low, dims, preferred_element_type=jnp.float32)

    def plane_copies(s, distance, kind):
        target = (plane + distance) % planes
        part = pl.ds(pl.multiple_of(target * share, share), share)
        source, landing = ((tile, tile_in), (flipped, flipped_in))[kind]
        return copy(
            source.at[s, :, :, part, :], landing.at[distance - 1, s],
            plane_send.at[kind, distance - 1, s], plane_recv.at[kind, distance - 1, s],
            {"pw": target},
        )

    def finish(s):
        def one(a, carry):
            n = acc.shape[2] // 2
            real = 2.0 * (acc[s, a, :n, :n] + acc[s, a, n:, n:])
            imag = 2.0 * (acc[s, a, :n, n:] - acc[s, a, n:, :n])
            tile[s, a, 0] = real
            tile[s, a, 1] = imag
            flipped[s, a, 0] = real.T
            flipped[s, a, 1] = -imag.T
            return carry

        lax.fori_loop(0, 4, one, 0)
        for distance in range(1, planes):
            plane_copies(s, distance, 0).start()

            @pl.when(s != z)
            def _():
                plane_copies(s, distance, 1).start()

    def place_near(chunk):
        return chunk + side * (rows - 1 - 2 * chunk)

    def place_far(chunk):
        return chunk + (1 - side) * (rows - 1 - 2 * chunk)

    for i in range(ahead):
        send_own(i)
        send_inward(i)

    def clear(i, carry):
        acc[i // 4, i % 4] = jnp.zeros(acc.shape[2:], jnp.float32)
        return carry

    lax.fori_loop(0, rows * 4, clear, 0)
    lag = mid - 1 - m

    def step(t, carry):
        v = t - lag
        inner_here = (v >= 0) & (v < cross_count)
        v = jnp.clip(v, 0, cross_count - 1)
        inner_chunk, inner_q = mid - 1 - v // half, v % half

        @pl.when(t < outer_count)
        def _():
            chunk, q = outer_arrival(t)
            arrived(same.at[chunk, q], same_recv.at[chunk, q])

        @pl.when(t + ahead < inner_sends)
        def _():
            send_inward(t + ahead)

        @pl.when(t + ahead < pieces)
        def _():
            send_own(t + ahead)

        @pl.when(inner_here)
        def _():
            arrived(other.at[inner_chunk, inner_q], other_recv.at[inner_chunk, inner_q])

        @pl.when(inner_here & (m > 0))
        def _():
            copy(
                other.at[inner_chunk, inner_q], other.at[inner_chunk, inner_q],
                out_send.at[v], other_recv.at[inner_chunk, inner_q], {"row": z_out},
            ).start()

        @pl.when(t < pieces)
        def _():
            q = order(t)
            arrived(panel.at[1, q], p_recv.at[1, q])
            copy(
                panel.at[1, q], panel.at[2, q], own_send.at[2, q], p_recv.at[2, q], {"col": core}
            ).start()
            arrived(panel.at[0, q], p_recv.at[0, q])

        @pl.when((t >= 1) & (t <= pieces))
        def _():
            q = order(t - 1)
            arrived(panel.at[2, q], p_recv.at[2, q])
            multiply(own(q), q, z)

            @pl.when(t == pieces)
            def _():
                finish(z)

        @pl.when((t >= half + 1) & (t - half - 1 < half * m))
        def _():
            chunk, q = outer_arrival(t - half - 1)
            multiply(same.at[chunk, q], q, place_near(chunk))

        @pl.when((t >= half * m) & (t < outer_count))
        def _():
            chunk, q = outer_arrival(t)
            multiply(same.at[chunk, q], q, place_near(chunk))

        w = t - 1 - lag

        @pl.when((w >= 0) & (w < cross_count))
        def _():
            chunk, q = mid - 1 - w // half, w % half
            multiply(other.at[chunk, q], q + half, place_far(chunk))

            @pl.when(q == half - 1)
            def _():
                finish(place_far(chunk))

        return carry

    steps = max(pieces + 1, cross_count + mid, 2 * half * (mid - 1))
    lax.fori_loop(0, steps, step, 0)

    def finish_near(chunk, carry):
        @pl.when(chunk < m)
        def _():
            finish(place_near(chunk))

        return carry

    lax.fori_loop(0, mid - 1, finish_near, 0)

    def gather(s, carry):
        far = s // mid != side
        m_of = s + side * (rows - 1 - 2 * s)
        mirrored = far | (m_of < m)
        here = pl.ds(pl.multiple_of(plane * share, share), share)

        @pl.when(mirrored | (s == z))
        def _():
            for distance in range(1, planes):
                plane_copies(s, distance, 0).wait()
            total = tile[s, :, :, here, :]
            for distance in range(1, planes):
                total += tile_in[distance - 1, s]
            direct_ref[s] = total

        @pl.when(mirrored)
        def _():
            for distance in range(1, planes):
                plane_copies(s, distance, 1).wait()
            total = flipped[s, :, :, here, :]
            for distance in range(1, planes):
                total += flipped_in[distance - 1, s]
            outgoing_ref[s] = total

        @pl.when(jnp.logical_not(mirrored))
        def _():
            outgoing_ref[s] = jnp.zeros(outgoing_ref.shape[1:], jnp.float32)

        @pl.when(jnp.logical_not(mirrored | (s == z)))
        def _():
            direct_ref[s] = jnp.zeros(direct_ref.shape[1:], jnp.float32)

        return carry

    lax.fori_loop(0, rows, gather, 0)

    def left(send):
        copy(own(0), panel.at[0, 0], send, p_recv.at[0, 0], {"col": core}).wait_send()

    def drain_own(i, carry):
        left(own_send.at[0, i])
        left(own_send.at[1, i])
        left(own_send.at[2, i])
        return carry

    lax.fori_loop(0, pieces, drain_own, 0)

    def drain_in(i, carry):
        @pl.when(i < inner_sends)
        def _():
            left(in_send.at[i])

        return carry

    lax.fori_loop(0, 2 * cross_count, drain_in, 0)

    @pl.when(m > 0)
    def _():
        def drain_out(i, carry):
            left(out_send.at[i])
            return carry

        lax.fori_loop(0, cross_count, drain_out, 0)


def summed_tiles(x, c, row_count, plane_count):
    _, length, depth = x.shape
    width = piece_width(depth)
    pieces, height = depth // width, 2 * length
    half, mid = pieces // 2, row_count // 2
    share = length // plane_count
    result = jax.ShapeDtypeStruct((row_count, 4, 2, share, length), jnp.float32)
    return pl.pallas_call(
        functools.partial(kernel, row_count, plane_count, pieces),
        out_shape=(result, result),
        in_specs=[pl.BlockSpec(memory_space=pltpu.VMEM)] * 2,
        out_specs=(pl.BlockSpec(memory_space=pltpu.VMEM),) * 2,
        scratch_shapes=[
            pltpu.VMEM((3, pieces, 2, length, width), jnp.float32),
            pltpu.VMEM((max(mid - 1, 1), pieces, 2, length, width), jnp.float32),
            pltpu.VMEM((mid, half, 2, length, width), jnp.float32),
            pltpu.VMEM((row_count, 4, height, height), jnp.float32),
            pltpu.VMEM((row_count, 4, 2, length, length), jnp.float32),
            pltpu.VMEM((row_count, 4, 2, length, length), jnp.float32),
            pltpu.VMEM((plane_count - 1, row_count, 4, 2, share, length), jnp.float32),
            pltpu.VMEM((plane_count - 1, row_count, 4, 2, share, length), jnp.float32),
            pltpu.SemaphoreType.DMA((3, pieces)),
            pltpu.SemaphoreType.DMA((max(mid - 1, 1), pieces)),
            pltpu.SemaphoreType.DMA((mid, half)),
            pltpu.SemaphoreType.DMA((3, pieces)),
            pltpu.SemaphoreType.DMA((2 * half * mid,)),
            pltpu.SemaphoreType.DMA((half * mid,)),
            pltpu.SemaphoreType.DMA((2, plane_count - 1, row_count)),
            pltpu.SemaphoreType.DMA((2, plane_count - 1, row_count)),
        ],
        compiler_params=pltpu.CompilerParams(
            collective_id=0, has_side_effects=True, vmem_limit_bytes=58 * 2**20
        ),
    )(x, c)


def per_device(
    pair_density, coulomb, valence_band, conduction_band, valence_energy, conduction_energy
):
    tile_len = pair_density.shape[0]
    row_count = lax.axis_size("row")
    col_count = lax.axis_size("col")
    plane_count = lax.axis_size("pw")
    share_len = tile_len // plane_count
    row_here = lax.axis_index("row")
    col_here = lax.axis_index("col")
    plane_here = lax.axis_index("pw")
    assert col_count == 4 and row_count % 2 == 0

    x = jnp.stack([pair_density[:, 0, :], pair_density[:, 1, :]]).astype(jnp.float32)
    c = coulomb[None, :]
    direct, outgoing = summed_tiles(x, c, row_count, plane_count)
    direct = jnp.transpose(direct, (1, 3, 2, 0, 4))
    outgoing = outgoing.reshape(row_count * col_count, 2, share_len, tile_len)
    incoming = lax.all_to_all(outgoing, ("row", "col"), split_axis=0, concat_axis=0, tiled=True)
    incoming = incoming.reshape(row_count, col_count, 2, share_len, tile_len)
    mirrored = jnp.transpose(incoming, (1, 3, 2, 0, 4))
    elsewhere = (jnp.arange(row_count, dtype=jnp.int32) != row_here)[None, None, None, :, None]
    reduced = direct + jnp.where(elsewhere, mirrored, 0.0)
    own_valence = lax.dynamic_slice_in_dim(valence_band, plane_here * share_len, share_len, 0)
    own_conduction = lax.dynamic_slice_in_dim(conduction_band, plane_here * share_len, share_len, 0)
    valence_ids = jnp.arange(valence_energy.shape[0], dtype=jnp.int32)
    conduction_ids = jnp.arange(conduction_energy.shape[0], dtype=jnp.int32)
    upper_level = jnp.sum(
        jnp.where(
            own_conduction[:, None] == conduction_ids[None, :], conduction_energy[None, :], 0.0
        ),
        axis=1,
    )
    lower_level = jnp.sum(
        jnp.where(own_valence[:, None] == valence_ids[None, :], valence_energy[None, :], 0.0),
        axis=1,
    )
    gap = upper_level - lower_level
    col_match = (jnp.arange(col_count, dtype=jnp.int32) == col_here)[:, None, None, None, None]
    row_match = (jnp.arange(row_count, dtype=jnp.int32) == row_here)[None, None, None, :, None]
    real_match = (jnp.arange(2, dtype=jnp.int32) == 0)[None, None, :, None, None]
    inner_match = (
        jnp.arange(tile_len, dtype=jnp.int32)[None, None, None, None, :]
        == plane_here * share_len
        + jnp.arange(share_len, dtype=jnp.int32)[None, :, None, None, None]
    )
    on_diagonal = col_match & row_match & real_match & inner_match
    result = reduced + jnp.where(on_diagonal, gap[None, :, None, None, None], 0.0)
    return result.reshape(1, col_count, share_len, 2, row_count, 1, tile_len)


def solution(mesh):
    placed = (
        P(("row", "col"), None, "pw"),
        P("pw"),
        P(("row", "col")),
        P(("row", "col")),
        P(),
        P(),
    )
    return jax.shard_map(
        per_device,
        mesh=mesh,
        in_specs=placed,
        out_specs=P("row", None, "pw", None, None, "col", None),
        check_vma=False,
    )
```

```python
import functools
import jax
import jax.numpy as jnp
from jax import lax
from jax.experimental import pallas as pl
from jax.experimental.pallas import tpu as pltpu
from jax.sharding import PartitionSpec as P

MESH = pl.DeviceIdType.MESH


def piece_width(depth):
    for width in (256,):
        if depth % (2 * width) == 0:
            return width
    return 128


def kernel(
    rows, planes, pieces, x_ref, c_ref, o_ref, panel, same, other, acc,
    tile, flipped, tile_in, flipped_in, outgoing, incoming,
    p_recv, same_recv, other_recv, own_send, in_send, out_send, plane_recv, plane_send,
    mirror_recv, mirror_send,
):
    half = pieces // 2
    mid = rows // 2
    ahead = min(2, half)
    z = lax.axis_index("row")
    b = lax.axis_index("col")
    core = b + 1 - 2 * (b % 2)
    beside = (b + 2) % 4
    opposite = 3 - b
    plane = lax.axis_index("pw")
    share = tile_in.shape[-2]
    side = z // mid
    m = z + side * (rows - 1 - 2 * z)
    step_in = 1 - 2 * side
    z_in = z + step_in
    z_out = z - step_in
    innermost = m == mid - 1
    cross_count = half * mid
    outer_count = 2 * half * m
    inner_sends = jnp.where(innermost, half * (m + 1), 2 * half * (m + 1))

    barrier = pltpu.get_barrier_semaphore()
    def greet(i, carry):
        other_one = (z * 4 + b + i) % (rows * 4)
        pl.semaphore_signal(
            barrier, inc=1, device_id={"row": other_one // 4, "col": other_one % 4},
            device_id_type=MESH,
        )
        return carry

    lax.fori_loop(1, rows * 4, greet, 0)
    for distance in range(1, planes):
        pl.semaphore_signal(
            barrier, inc=1, device_id={"pw": (plane + distance) % planes}, device_id_type=MESH
        )
    pl.semaphore_wait(barrier, rows * 4 + planes - 2)

    def copy(src, dst, send, recv, where):
        return pltpu.make_async_remote_copy(
            src_ref=src, dst_ref=dst, send_sem=send, recv_sem=recv,
            device_id=where, device_id_type=MESH,
        )

    def arrived(slot, recv):
        copy(slot, slot, own_send.at[0, 0], recv, {"col": core}).wait_recv()

    def order(i):
        return (i + half) % pieces

    def span(q):
        width = panel.shape[-1]
        place = (q + side * half) % pieces
        return pl.ds(pl.multiple_of(place * width, 128), width)

    def own(q):
        return x_ref.at[:, :, span(q)]

    def send_own(i):
        q = order(i)
        copy(own(q), panel.at[0, q], own_send.at[0, q], p_recv.at[0, q], {"col": core}).start()
        copy(own(q), panel.at[1, q], own_send.at[1, q], p_recv.at[1, q], {"col": beside}).start()

    def send_inward(s):
        crossing = s < half * (m + 1)
        rest = jnp.where(crossing, s, s - half * (m + 1))
        back = rest // half
        chunk = m - back
        q = rest % half + jnp.where(crossing, 0, half)
        where = {"row": z_in}

        @pl.when(innermost & (back == 0))
        def _():
            copy(own(q), other.at[chunk, q], in_send.at[s], other_recv.at[chunk, q], where).start()

        @pl.when(innermost & (back > 0))
        def _():
            copy(same.at[chunk, q], other.at[chunk, q], in_send.at[s], other_recv.at[chunk, q], where).start()

        @pl.when(jnp.logical_not(innermost) & (back == 0))
        def _():
            copy(own(q), same.at[chunk, q], in_send.at[s], same_recv.at[chunk, q], where).start()

        if mid > 2:
            @pl.when(jnp.logical_not(innermost) & (back > 0))
            def _():
                copy(same.at[chunk, q], same.at[chunk, q], in_send.at[s], same_recv.at[chunk, q], where).start()

    def outer_arrival(u):
        crossing = u < half * m
        rest = jnp.where(crossing, u, u - half * m)
        return m - 1 - rest // half, rest % half + jnp.where(crossing, 0, half)

    def multiply(chunk, q, target):
        weighted = chunk[...].reshape(acc.shape[2], -1) * c_ref[:, span(q)]
        high = weighted.astype(jnp.bfloat16)
        low = (weighted - high.astype(jnp.float32)).astype(jnp.bfloat16)
        blocks = (own(q), panel.at[0, q], panel.at[1, q], panel.at[2, q])
        dims = (((1,), (1,)), ((), ()))
        for block, a in zip(blocks, (b, core, beside, opposite)):
            left = block[...].reshape(acc.shape[2], -1).astype(jnp.bfloat16)
            acc[target, a] += lax.dot_general(
                left, high, dims, preferred_element_type=jnp.float32
            ) + lax.dot_general(left, low, dims, preferred_element_type=jnp.float32)

    def plane_copies(s, distance, kind):
        target = (plane + distance) % planes
        part = pl.ds(pl.multiple_of(target * share, share), share)
        source, landing = ((tile, tile_in), (flipped, flipped_in))[kind]
        return copy(
            source.at[s, :, :, part, :], landing.at[distance - 1, s],
            plane_send.at[kind, distance - 1, s], plane_recv.at[kind, distance - 1, s],
            {"pw": target},
        )

    def finish(s):
        def one(a, carry):
            n = acc.shape[2] // 2
            real = 2.0 * (acc[s, a, :n, :n] + acc[s, a, n:, n:])
            imag = 2.0 * (acc[s, a, :n, n:] - acc[s, a, n:, :n])
            tile[s, a, 0] = real
            tile[s, a, 1] = imag
            flipped[s, a, 0] = real.T
            flipped[s, a, 1] = -imag.T
            return carry

        lax.fori_loop(0, 4, one, 0)

        @pl.when(s != z)
        def _():
            for distance in range(1, planes):
                plane_copies(s, distance, 1).start()

    def send_direct(s):
        for distance in range(1, planes):
            plane_copies(s, distance, 0).start()

    def place_near(chunk):
        return chunk + side * (rows - 1 - 2 * chunk)

    def place_far(chunk):
        return chunk + (1 - side) * (rows - 1 - 2 * chunk)

    for i in range(ahead):
        send_own(i)
        send_inward(i)

    def clear(i, carry):
        acc[i // 4, i % 4] = jnp.zeros(acc.shape[2:], jnp.float32)
        return carry

    lax.fori_loop(0, rows * 4, clear, 0)
    lag = mid - 1 - m

    def step(t, carry):
        v = t - lag
        inner_here = (v >= 0) & (v < cross_count)
        v = jnp.clip(v, 0, cross_count - 1)
        inner_chunk, inner_q = mid - 1 - v // half, v % half

        @pl.when(t < outer_count)
        def _():
            chunk, q = outer_arrival(t)
            arrived(same.at[chunk, q], same_recv.at[chunk, q])

        @pl.when(t + ahead < inner_sends)
        def _():
            send_inward(t + ahead)

        @pl.when(t + ahead < pieces)
        def _():
            send_own(t + ahead)

        @pl.when(inner_here)
        def _():
            arrived(other.at[inner_chunk, inner_q], other_recv.at[inner_chunk, inner_q])

        @pl.when(inner_here & (m > 0))
        def _():
            copy(
                other.at[inner_chunk, inner_q], other.at[inner_chunk, inner_q],
                out_send.at[v], other_recv.at[inner_chunk, inner_q], {"row": z_out},
            ).start()

        @pl.when(t < pieces)
        def _():
            q = order(t)
            arrived(panel.at[1, q], p_recv.at[1, q])
            copy(
                panel.at[1, q], panel.at[2, q], own_send.at[2, q], p_recv.at[2, q], {"col": core}
            ).start()
            arrived(panel.at[0, q], p_recv.at[0, q])

        @pl.when((t >= 1) & (t <= pieces))
        def _():
            q = order(t - 1)
            arrived(panel.at[2, q], p_recv.at[2, q])
            multiply(own(q), q, z)

            @pl.when(t == pieces)
            def _():
                finish(z)

        @pl.when((t >= half + 1) & (t - half - 1 < half * m))
        def _():
            chunk, q = outer_arrival(t - half - 1)
            multiply(same.at[chunk, q], q, place_near(chunk))

        @pl.when((t >= half * m) & (t < outer_count))
        def _():
            chunk, q = outer_arrival(t)
            multiply(same.at[chunk, q], q, place_near(chunk))

        w = t - 1 - lag

        @pl.when((w >= 0) & (w < cross_count))
        def _():
            chunk, q = mid - 1 - w // half, w % half
            multiply(other.at[chunk, q], q + half, place_far(chunk))

            @pl.when(q == half - 1)
            def _():
                finish(place_far(chunk))

                @pl.when(chunk > 0)
                def _():
                    send_direct(place_far(chunk))

        return carry

    steps = max(pieces + 1, cross_count + mid, 2 * half * (mid - 1))
    lax.fori_loop(0, steps, step, 0)

    def finish_near(chunk, carry):
        @pl.when(chunk < m)
        def _():
            finish(place_near(chunk))

        return carry

    lax.fori_loop(0, mid - 1, finish_near, 0)

    send_direct(place_far(0))
    send_direct(z)

    def direct_near(chunk, carry):
        @pl.when(chunk < m)
        def _():
            send_direct(place_near(chunk))

        return carry

    lax.fori_loop(0, mid - 1, direct_near, 0)
    here = pl.ds(pl.multiple_of(plane * share, share), share)

    def mirror_copy(s, a):
        return copy(
            outgoing.at[s, a], incoming.at[z, b], mirror_send.at[s, a], mirror_recv.at[z, b],
            {"row": s, "col": a},
        )

    def send_mirrored(s):
        for distance in range(1, planes):
            plane_copies(s, distance, 1).wait()
        total = flipped[s, :, :, here, :]
        for distance in range(1, planes):
            total += flipped_in[distance - 1, s]
        outgoing[s] = total

        def one(a, carry):
            mirror_copy(s, a).start()
            return carry

        lax.fori_loop(0, 4, one, 0)

    def mirror_far(i, carry):
        send_mirrored(place_far(mid - 1 - i))
        return carry

    lax.fori_loop(0, mid, mirror_far, 0)

    def mirror_near(chunk, carry):
        @pl.when(chunk < m)
        def _():
            send_mirrored(place_near(chunk))

        return carry

    lax.fori_loop(0, mid - 1, mirror_near, 0)

    def gather(s, carry):
        far = s // mid != side
        m_of = s + side * (rows - 1 - 2 * s)
        computed = far | (m_of <= m)

        @pl.when(computed)
        def _():
            for distance in range(1, planes):
                plane_copies(s, distance, 0).wait()
            total = tile[s, :, :, here, :]
            for distance in range(1, planes):
                total += tile_in[distance - 1, s]
            o_ref[s] = total

        @pl.when(jnp.logical_not(computed))
        def _():
            o_ref[s] = jnp.zeros(o_ref.shape[1:], jnp.float32)

        return carry

    lax.fori_loop(0, rows, gather, 0)

    def receive(i, carry):
        s, a = i // 4, i % 4
        far = s // mid != side
        m_of = s + side * (rows - 1 - 2 * s)

        @pl.when(far | (m_of > m))
        def _():
            arrived(incoming.at[s, a], mirror_recv.at[s, a])
            o_ref[s, a] += incoming[s, a]

        return carry

    lax.fori_loop(0, rows * 4, receive, 0)

    def drain_mirror(i, carry):
        s, a = i // 4, i % 4
        far = s // mid != side
        m_of = s + side * (rows - 1 - 2 * s)

        @pl.when(far | (m_of < m))
        def _():
            mirror_copy(s, a).wait_send()

        return carry

    lax.fori_loop(0, rows * 4, drain_mirror, 0)

    def left(send):
        copy(own(0), panel.at[0, 0], send, p_recv.at[0, 0], {"col": core}).wait_send()

    def drain_own(i, carry):
        left(own_send.at[0, i])
        left(own_send.at[1, i])
        left(own_send.at[2, i])
        return carry

    lax.fori_loop(0, pieces, drain_own, 0)

    def drain_in(i, carry):
        @pl.when(i < inner_sends)
        def _():
            left(in_send.at[i])

        return carry

    lax.fori_loop(0, 2 * cross_count, drain_in, 0)

    @pl.when(m > 0)
    def _():
        def drain_out(i, carry):
            left(out_send.at[i])
            return carry

        lax.fori_loop(0, cross_count, drain_out, 0)


def summed_tiles(x, c, row_count, plane_count):
    _, length, depth = x.shape
    width = piece_width(depth)
    pieces, height = depth // width, 2 * length
    half, mid = pieces // 2, row_count // 2
    share = length // plane_count
    result = jax.ShapeDtypeStruct((row_count, 4, 2, share, length), jnp.float32)
    return pl.pallas_call(
        functools.partial(kernel, row_count, plane_count, pieces),
        out_shape=result,
        in_specs=[pl.BlockSpec(memory_space=pltpu.VMEM)] * 2,
        out_specs=pl.BlockSpec(memory_space=pltpu.VMEM),
        scratch_shapes=[
            pltpu.VMEM((3, pieces, 2, length, width), jnp.float32),
            pltpu.VMEM((max(mid - 1, 1), pieces, 2, length, width), jnp.float32),
            pltpu.VMEM((mid, half, 2, length, width), jnp.float32),
            pltpu.VMEM((row_count, 4, height, height), jnp.float32),
            pltpu.VMEM((row_count, 4, 2, length, length), jnp.float32),
            pltpu.VMEM((row_count, 4, 2, length, length), jnp.float32),
            pltpu.VMEM((plane_count - 1, row_count, 4, 2, share, length), jnp.float32),
            pltpu.VMEM((plane_count - 1, row_count, 4, 2, share, length), jnp.float32),
            pltpu.VMEM((row_count, 4, 2, share, length), jnp.float32),
            pltpu.VMEM((row_count, 4, 2, share, length), jnp.float32),
            pltpu.SemaphoreType.DMA((3, pieces)),
            pltpu.SemaphoreType.DMA((max(mid - 1, 1), pieces)),
            pltpu.SemaphoreType.DMA((mid, half)),
            pltpu.SemaphoreType.DMA((3, pieces)),
            pltpu.SemaphoreType.DMA((2 * half * mid,)),
            pltpu.SemaphoreType.DMA((half * mid,)),
            pltpu.SemaphoreType.DMA((2, plane_count - 1, row_count)),
            pltpu.SemaphoreType.DMA((2, plane_count - 1, row_count)),
            pltpu.SemaphoreType.DMA((row_count, 4)),
            pltpu.SemaphoreType.DMA((row_count, 4)),
        ],
        compiler_params=pltpu.CompilerParams(
            collective_id=0, has_side_effects=True, vmem_limit_bytes=58 * 2**20
        ),
    )(x, c)


def per_device(
    pair_density, coulomb, valence_band, conduction_band, valence_energy, conduction_energy
):
    tile_len = pair_density.shape[0]
    row_count = lax.axis_size("row")
    col_count = lax.axis_size("col")
    plane_count = lax.axis_size("pw")
    share_len = tile_len // plane_count
    row_here = lax.axis_index("row")
    col_here = lax.axis_index("col")
    plane_here = lax.axis_index("pw")
    assert col_count == 4 and row_count % 2 == 0

    x = jnp.stack([pair_density[:, 0, :], pair_density[:, 1, :]]).astype(jnp.float32)
    c = coulomb[None, :]
    reduced = jnp.transpose(summed_tiles(x, c, row_count, plane_count), (1, 3, 2, 0, 4))
    own_valence = lax.dynamic_slice_in_dim(valence_band, plane_here * share_len, share_len, 0)
    own_conduction = lax.dynamic_slice_in_dim(conduction_band, plane_here * share_len, share_len, 0)
    valence_ids = jnp.arange(valence_energy.shape[0], dtype=jnp.int32)
    conduction_ids = jnp.arange(conduction_energy.shape[0], dtype=jnp.int32)
    upper_level = jnp.sum(
        jnp.where(
            own_conduction[:, None] == conduction_ids[None, :], conduction_energy[None, :], 0.0
        ),
        axis=1,
    )
    lower_level = jnp.sum(
        jnp.where(own_valence[:, None] == valence_ids[None, :], valence_energy[None, :], 0.0),
        axis=1,
    )
    gap = upper_level - lower_level
    col_match = (jnp.arange(col_count, dtype=jnp.int32) == col_here)[:, None, None, None, None]
    row_match = (jnp.arange(row_count, dtype=jnp.int32) == row_here)[None, None, None, :, None]
    real_match = (jnp.arange(2, dtype=jnp.int32) == 0)[None, None, :, None, None]
    inner_match = (
        jnp.arange(tile_len, dtype=jnp.int32)[None, None, None, None, :]
        == plane_here * share_len
        + jnp.arange(share_len, dtype=jnp.int32)[None, :, None, None, None]
    )
    on_diagonal = col_match & row_match & real_match & inner_match
    result = reduced + jnp.where(on_diagonal, gap[None, :, None, None, None], 0.0)
    return result.reshape(1, col_count, share_len, 2, row_count, 1, tile_len)


def solution(mesh):
    placed = (
        P(("row", "col"), None, "pw"),
        P("pw"),
        P(("row", "col")),
        P(("row", "col")),
        P(),
        P(),
    )
    return jax.shard_map(
        per_device,
        mesh=mesh,
        in_specs=placed,
        out_specs=P("row", None, "pw", None, None, "col", None),
        check_vma=False,
    )
```
